32 devices in a mesh: chan: 4 (over z), tm: 8 (over y, x, core).
Axes of the slice: x: 2, y: 2, z: 4, core: 2. Of those that a mesh axis runs over, the one named last changes fastest.
Arguments:
- raw_strain: float32 [256, 8192], P('chan', 'tm'), may hold values from -6 to 6
- whitening: float32 [1024], replicated, may hold values from -0.1875 to 0.1875
- block_mask: int32 [4, 4], replicated, may hold values from 0 to 1, as said below
- old_stack: float32 [32, 256, 256], P('tm', 'chan'), may hold values from -6 to 6
Outputs:
- new_stack: float32 [32, 256, 256], P('tm', 'chan')
The draws below stay inside these ranges and needn't reach their ends.
Inputs may be any that keep to these rules, and one draw needn't show every extreme that they name: block_mask[a, b] is 1 exactly where (b - a) mod 4 is below a reach of row a, each reach at least 1, and 0 elsewhere.
All inputs are finite; a program needn't handle non-finite values.
Results may differ from the reference program's by a relative error of at most 0.0018.
Values may be sent and summed in bfloat16 or wider, within the bound.
A program may use at most 64 MiB of HBM per device.

```python
import jax
import jax.numpy as jnp
from jax import lax

BLOCK = 64
K = 1024
LAGS = 32
CHANNELS = 256
SAMPLES = 8192
NBLK = 4


def draw_block_mask(key, part):
    reaches = jax.random.randint(key, (NBLK,), 1, NBLK + 1)
    counter = jnp.arange(NBLK, dtype=jnp.int32)
    reaches = jnp.where(counter == 0, 1, reaches)
    offsets = (counter[None, :] - counter[:, None]) % NBLK
    return (offsets < reaches[:, None]).astype(jnp.int32)


def steps_of(own_key, shape, split, smallest, top_value):
    gain, own = 1.0, jax.random.fold_in(own_key, 6)
    for dim, shards_of in split:
        draws = jnp.exp(jax.random.uniform(jax.random.fold_in(own, dim), (shards_of,), jnp.float32, smallest / len(split), top_value / len(split)))
        gain = gain * jnp.repeat(draws, shape[dim] // shards_of).reshape([-1 if axis == dim else 1 for axis in range(len(shape))])
    return gain


def scatter_about(rng, dims, width, bound, shards=(), kind=jnp.bfloat16):
    gain = steps_of(rng, dims, shards, -0.22, 0.18) if shards else 1.0
    result = jax.random.normal(rng, dims, jnp.float32) * width * gain
    return jnp.minimum(jnp.maximum(result, -bound), bound).astype(kind)


def setup_inputs(seed: int = 0) -> dict:
    splits = jax.random.split(jax.random.key(seed), 5)
    return {
        "raw_strain": scatter_about(splits[0], (CHANNELS, SAMPLES), 1.0, 6.0, ((0, 4), (1, 8)), jnp.float32),
        "whitening": scatter_about(splits[1], (K,), K ** -0.5, 0.1875, (), jnp.float32),
        "block_mask": draw_block_mask(jax.random.fold_in(splits[4], 71), 0),
        "old_stack": scatter_about(splits[3], (LAGS, CHANNELS, CHANNELS), 1.0, 6.0, ((0, 8), (1, 4)), jnp.float32),
    }


def reference(raw_strain, whitening, block_mask, old_stack):
    samples = raw_strain.shape[1]
    fft_len = samples + 2 * K
    padded = jnp.pad(raw_strain, ((0, 0), (K // 2, K // 2)))
    spectrum = jnp.conj(jnp.fft.rfft(whitening, fft_len)) * jnp.fft.rfft(padded, fft_len, axis=1)
    filtered = jnp.fft.irfft(spectrum, fft_len, axis=1)[:, :samples].astype(jnp.bfloat16)
    wide_data = filtered.astype(jnp.float32)
    extended = jnp.pad(wide_data, ((0, 0), (0, LAGS)))

    def one_lag(offset):
        shifted = lax.dynamic_slice_in_dim(extended, offset, samples, 1)
        return jnp.dot(wide_data, shifted.T, preferred_element_type=jnp.float32)

    lagged = lax.map(one_lag, jnp.arange(LAGS, dtype=jnp.int32))
    weights = jnp.repeat(jnp.repeat(block_mask, BLOCK, axis=0), BLOCK, axis=1).astype(jnp.float32)
    scaling = float(samples) ** -0.5
    return old_stack + (lagged * weights[None, :, :]) * scaling
```

```python
import functools

import jax
import jax.numpy as jnp
from jax import lax
from jax.experimental import pallas as pl
from jax.experimental.pallas import tpu as pltpu
from jax.sharding import PartitionSpec as P

MESH = pl.DeviceIdType.MESH
LANES = 128
NT = (((1,), (1,)), ((), ()))


def toeplitz_kernel(taps_ref, high_ref, both_ref):
    rows, width = high_ref.shape
    spread = jnp.broadcast_to(taps_ref[...], (rows, width))
    matrix = pltpu.roll(spread, 0, 1, stride=1, stride_axis=0)
    high = matrix.astype(jnp.bfloat16)
    low = (matrix - high.astype(jnp.float32)).astype(jnp.bfloat16)
    high_ref[...] = high
    both_ref[:rows] = high
    both_ref[rows:] = low


def toeplitz(whitening):
    width = whitening.shape[0] + LANES
    taps = jnp.pad(whitening, (0, LANES)).reshape(1, width)
    return pl.pallas_call(
        toeplitz_kernel,
        out_shape=(
            jax.ShapeDtypeStruct((LANES, width), jnp.bfloat16),
            jax.ShapeDtypeStruct((2 * LANES, width), jnp.bfloat16),
        ),
    )(taps)


def main_kernel(
    n_chan, n_tm, lag_total, half, left,
    raw_ref, high_ref, both_ref, out_ref,
    low_halo, high_halo, win_high, win_low, wide, stack, blocks, part, near, sent, far,
    halo_send, halo_recv, gather_send, gather_recv, near_send, near_recv, far_send, far_recv,
):
    chan, tm = lax.axis_index("chan"), lax.axis_index("tm")
    channels, seg = raw_ref.shape
    chips = n_tm // 2
    chip, core = tm // 2, lax.rem(tm, 2)
    lag_rows = channels * (lag_total // n_tm)

    barrier = pltpu.get_barrier_semaphore()
    for d in range(1, n_tm):
        pl.semaphore_signal(
            barrier, inc=1, device_id=(chan, lax.rem(tm + d, n_tm)), device_id_type=MESH
        )
    for d in range(1, n_chan):
        pl.semaphore_signal(
            barrier, inc=1, device_id=(lax.rem(chan + d, n_chan), tm), device_id_type=MESH
        )
    pl.semaphore_wait(barrier, n_tm - 1 + n_chan - 1)

    to_right = pltpu.make_async_remote_copy(
        src_ref=raw_ref.at[:, pl.ds(seg - half - left, half + left)],
        dst_ref=low_halo,
        send_sem=halo_send.at[0],
        recv_sem=halo_recv.at[0],
        device_id=(chan, lax.rem(tm + 1, n_tm)),
        device_id_type=MESH,
    )
    to_left = pltpu.make_async_remote_copy(
        src_ref=raw_ref.at[:, pl.ds(0, half)],
        dst_ref=high_halo,
        send_sem=halo_send.at[1],
        recv_sem=halo_recv.at[1],
        device_id=(chan, lax.rem(tm + n_tm - 1, n_tm)),
        device_id_type=MESH,
    )
    to_right.start()
    to_left.start()
    to_right.wait_recv()
    to_left.wait_recv()
    not_first = (tm > 0).astype(jnp.float32)
    not_last = (tm < n_tm - 1).astype(jnp.float32)
    padded = jnp.concatenate(
        [low_halo[...] * not_first, raw_ref[...], high_halo[...] * not_last], axis=1
    )
    high = padded.astype(jnp.bfloat16)
    low = (padded - high.astype(jnp.float32)).astype(jnp.bfloat16)
    pieces = (seg + left) // LANES
    width = 2 * half + LANES
    for b in range(pieces):
        win_high[pl.ds(b * channels, channels)] = high[:, b * LANES : b * LANES + width]
        win_low[pl.ds(b * channels, channels)] = low[:, b * LANES : b * LANES + width]
    both = lax.dot_general(
        win_high[...], both_ref[...], NT, preferred_element_type=jnp.float32
    )
    rest = lax.dot_general(
        win_low[...], high_ref[...], NT, preferred_element_type=jnp.float32
    )
    total = both[:, :LANES] + (both[:, LANES:] + rest)
    rounded = total.astype(jnp.bfloat16)
    ahead = left // LANES
    for b in range(ahead, pieces):
        blocks[chan, :, pl.ds((b - ahead) * LANES, LANES)] = rounded[
            b * channels : (b + 1) * channels
        ]

    gathers = []
    for d in range(1, n_chan):
        gathers.append(
            pltpu.make_async_remote_copy(
                src_ref=blocks.at[chan],
                dst_ref=blocks.at[chan],
                send_sem=gather_send.at[d],
                recv_sem=gather_recv.at[d],
                device_id=(lax.rem(chan + d, n_chan), tm),
                device_id_type=MESH,
            )
        )
        gathers[-1].start()

    exact = rounded.astype(jnp.float32)
    for b in range(pieces):
        piece = exact[b * channels : (b + 1) * channels]
        wide[:, pl.ds(b * LANES, LANES)] = piece * not_first if b < ahead else piece
    for lag in range(lag_total):
        q, row = divmod(lag * channels, lag_rows)
        moved = wide[...] if lag == 0 else pltpu.roll(wide[...], lag, 1)
        stack[q, pl.ds(row, channels)] = moved[:, left:].astype(jnp.bfloat16)
    for copy in gathers:
        copy.wait_recv()

    partner = blocks[...].reshape(n_chan * channels, seg)

    def partial_sums(q):
        return lax.dot_general(stack[q], partner, NT, preferred_element_type=jnp.float32)

    near_copies = []
    for d in range(chips):
        owner = lax.rem(chip + d + 1, chips)
        part[d] = partial_sums(owner * 2 + 1 - core)
        near_copies.append(
            pltpu.make_async_remote_copy(
                src_ref=part.at[d],
                dst_ref=near.at[d],
                send_sem=near_send.at[d],
                recv_sem=near_recv.at[d],
                device_id=(chan, chip * 2 + 1 - core),
                device_id_type=MESH,
            )
        )
        near_copies[-1].start()
    far_copies = []
    for d in range(chips - 1):
        owner = lax.rem(chip + d + 1, chips)
        own = partial_sums(owner * 2 + core)
        near_copies[d].wait_recv()
        sent[d] = (own + near[d]).astype(jnp.bfloat16)
        far_copies.append(
            pltpu.make_async_remote_copy(
                src_ref=sent.at[d],
                dst_ref=far.at[d],
                send_sem=far_send.at[d],
                recv_sem=far_recv.at[d],
                device_id=(chan, owner * 2 + core),
                device_id_type=MESH,
            )
        )
        far_copies[-1].start()
    own = partial_sums(chip * 2 + core)
    near_copies[chips - 1].wait_recv()
    own = own + near[chips - 1]
    for d in range(chips - 1):
        far_copies[d].wait_recv()
        own = own + far[d].astype(jnp.float32)
    out_ref[...] = own

    to_right.wait_send()
    to_left.wait_send()
    for copy in gathers + near_copies + far_copies:
        copy.wait_send()


def shards(n_chan, n_tm, raw_strain, whitening, block_mask, old_stack):
    channels, seg = raw_strain.shape
    taps = whitening.shape[0]
    half = taps // 2
    lags = old_stack.shape[0]
    lag_total = lags * n_tm
    left = -(-lag_total // LANES) * LANES
    chips = n_tm // 2
    rows = channels * lags
    every = n_chan * channels
    width = taps + LANES
    windows = channels * (seg + left) // LANES
    high, both = toeplitz(whitening)
    dma = pltpu.SemaphoreType.DMA
    sums = pl.pallas_call(
        functools.partial(main_kernel, n_chan, n_tm, lag_total, half, left),
        out_shape=jax.ShapeDtypeStruct((rows, every), jnp.float32),
        in_specs=[pl.BlockSpec(memory_space=pltpu.VMEM)] * 3,
        out_specs=pl.BlockSpec(memory_space=pltpu.VMEM),
        scratch_shapes=[
            pltpu.VMEM((channels, half + left), jnp.float32),
            pltpu.VMEM((channels, half), jnp.float32),
            pltpu.VMEM((windows, width), jnp.bfloat16),
            pltpu.VMEM((windows, width), jnp.bfloat16),
            pltpu.VMEM((channels, seg + left), jnp.float32),
            pltpu.VMEM((n_tm, rows, seg), jnp.bfloat16),
            pltpu.VMEM((n_chan, channels, seg), jnp.bfloat16),
            pltpu.VMEM((chips, rows, every), jnp.float32),
            pltpu.VMEM((chips, rows, every), jnp.float32),
            pltpu.VMEM((chips, rows, every), jnp.bfloat16),
            pltpu.VMEM((chips, rows, every), jnp.bfloat16),
            dma((2,)),
            dma((2,)),
            dma((n_chan,)),
            dma((n_chan,)),
            dma((chips,)),
            dma((chips,)),
            dma((chips,)),
            dma((chips,)),
        ],
        compiler_params=pltpu.CompilerParams(
            collective_id=0, has_side_effects=True, vmem_limit_bytes=40 * 1024 * 1024
        ),
    )(raw_strain, high, both)
    scaling = float(seg * n_tm) ** (-0.5)
    mask_row = lax.dynamic_index_in_dim(block_mask, lax.axis_index("chan"), 0, keepdims=False)
    weights = jnp.repeat(mask_row.astype(jnp.float32) * scaling, channels)
    return old_stack + sums.reshape(lags, channels, every) * weights


def solution(mesh):
    body = functools.partial(shards, mesh.shape["chan"], mesh.shape["tm"])
    in_specs = (P("chan", "tm"), P(), P(), P("tm", "chan", None))
    out_specs = P("tm", "chan", None)
    return jax.shard_map(body, mesh=mesh, in_specs=in_specs, out_specs=out_specs, check_vma=False)
```

```python
import functools

import jax
import jax.numpy as jnp
from jax import lax
from jax.experimental import pallas as pl
from jax.experimental.pallas import tpu as pltpu
from jax.sharding import PartitionSpec as P

MESH = pl.DeviceIdType.MESH
LANES = 128
NT = (((1,), (1,)), ((), ()))


def main_kernel(
    n_chan, n_tm, lag_total, half, left,
    raw_ref, taps_ref, mask_ref, out_ref,
    local, low_halo, high_halo, win_high, win_low, wide, stack, blocks, part, near, sent, far,
    local_sem, halo_send, halo_recv, gather_send, gather_recv, near_send, near_recv, far_send, far_recv,
):
    chan, tm = lax.axis_index("chan"), lax.axis_index("tm")
    channels, seg = raw_ref.shape
    chips = n_tm // 2
    chip, core = tm // 2, lax.rem(tm, 2)
    lag_rows = channels * (lag_total // n_tm)

    own_copy = pltpu.make_async_copy(raw_ref, local, local_sem)
    own_copy.start()
    barrier = pltpu.get_barrier_semaphore()
    for d in range(1, n_tm):
        pl.semaphore_signal(
            barrier, inc=1, device_id=(chan, lax.rem(tm + d, n_tm)), device_id_type=MESH
        )
    for d in range(1, n_chan):
        pl.semaphore_signal(
            barrier, inc=1, device_id=(lax.rem(chan + d, n_chan), tm), device_id_type=MESH
        )
    pl.semaphore_wait(barrier, n_tm - 1 + n_chan - 1)

    to_right = pltpu.make_async_remote_copy(
        src_ref=raw_ref.at[:, pl.ds(seg - half - left, half + left)],
        dst_ref=low_halo,
        send_sem=halo_send.at[0],
        recv_sem=halo_recv.at[0],
        device_id=(chan, lax.rem(tm + 1, n_tm)),
        device_id_type=MESH,
    )
    to_left = pltpu.make_async_remote_copy(
        src_ref=raw_ref.at[:, pl.ds(0, half)],
        dst_ref=high_halo,
        send_sem=halo_send.at[1],
        recv_sem=halo_recv.at[1],
        device_id=(chan, lax.rem(tm + n_tm - 1, n_tm)),
        device_id_type=MESH,
    )
    to_right.start()
    to_left.start()

    width = 2 * half + LANES
    taps = jnp.concatenate(
        [taps_ref[...].reshape(1, 2 * half), jnp.zeros((1, LANES), jnp.float32)], axis=1
    )
    matrix = pltpu.roll(
        jnp.broadcast_to(taps, (LANES, width)), 0, 1, stride=1, stride_axis=0
    )
    matrix_high = matrix.astype(jnp.bfloat16)
    matrix_low = (matrix - matrix_high.astype(jnp.float32)).astype(jnp.bfloat16)
    matrix_both = jnp.concatenate([matrix_high, matrix_low], axis=0)

    own_copy.wait()
    to_right.wait_recv()
    to_left.wait_recv()
    not_first = (tm > 0).astype(jnp.float32)
    not_last = (tm < n_tm - 1).astype(jnp.float32)
    padded = jnp.concatenate(
        [low_halo[...] * not_first, local[...], high_halo[...] * not_last], axis=1
    )
    high = padded.astype(jnp.bfloat16)
    low = (padded - high.astype(jnp.float32)).astype(jnp.bfloat16)
    pieces = (seg + left) // LANES
    for b in range(pieces):
        win_high[pl.ds(b * channels, channels)] = high[:, b * LANES : b * LANES + width]
        win_low[pl.ds(b * channels, channels)] = low[:, b * LANES : b * LANES + width]
    both = lax.dot_general(
        win_high[...], matrix_both, NT, preferred_element_type=jnp.float32
    )
    rest = lax.dot_general(
        win_low[...], matrix_high, NT, preferred_element_type=jnp.float32
    )
    total = both[:, :LANES] + (both[:, LANES:] + rest)
    rounded = total.astype(jnp.bfloat16)
    ahead = left // LANES
    for b in range(ahead, pieces):
        blocks[chan, :, pl.ds((b - ahead) * LANES, LANES)] = rounded[
            b * channels : (b + 1) * channels
        ]

    gathers = []
    for d in range(1, n_chan):
        gathers.append(
            pltpu.make_async_remote_copy(
                src_ref=blocks.at[chan],
                dst_ref=blocks.at[chan],
                send_sem=gather_send.at[d],
                recv_sem=gather_recv.at[d],
                device_id=(lax.rem(chan + d, n_chan), tm),
                device_id_type=MESH,
            )
        )
        gathers[-1].start()

    exact = rounded.astype(jnp.float32)
    for b in range(pieces):
        piece = exact[b * channels : (b + 1) * channels]
        wide[:, pl.ds(b * LANES, LANES)] = piece * not_first if b < ahead else piece
    for lag in range(lag_total):
        q, row = divmod(lag * channels, lag_rows)
        moved = wide[...] if lag == 0 else pltpu.roll(wide[...], lag, 1)
        stack[q, pl.ds(row, channels)] = moved[:, left:].astype(jnp.bfloat16)
    for copy in gathers:
        copy.wait_recv()

    partner = blocks[...].reshape(n_chan * channels, seg)

    def partial_sums(q):
        return lax.dot_general(stack[q], partner, NT, preferred_element_type=jnp.float32)

    near_copies = []
    for d in range(chips):
        owner = lax.rem(chip + d + 1, chips)
        part[d] = partial_sums(owner * 2 + 1 - core)
        near_copies.append(
            pltpu.make_async_remote_copy(
                src_ref=part.at[d],
                dst_ref=near.at[d],
                send_sem=near_send.at[d],
                recv_sem=near_recv.at[d],
                device_id=(chan, chip * 2 + 1 - core),
                device_id_type=MESH,
            )
        )
        near_copies[-1].start()
    far_copies = []
    for d in range(chips - 1):
        owner = lax.rem(chip + d + 1, chips)
        own = partial_sums(owner * 2 + core)
        near_copies[d].wait_recv()
        sent[d] = (own + near[d]).astype(jnp.bfloat16)
        far_copies.append(
            pltpu.make_async_remote_copy(
                src_ref=sent.at[d],
                dst_ref=far.at[d],
                send_sem=far_send.at[d],
                recv_sem=far_recv.at[d],
                device_id=(chan, owner * 2 + core),
                device_id_type=MESH,
            )
        )
        far_copies[-1].start()
    own = partial_sums(chip * 2 + core)
    near_copies[chips - 1].wait_recv()
    own = own + near[chips - 1]
    for d in range(chips - 1):
        far_copies[d].wait_recv()
        own = own + far[d].astype(jnp.float32)
    place = lax.broadcasted_iota(jnp.int32, (1, n_chan * channels), 1)
    weights = jnp.zeros((1, n_chan * channels), jnp.float32)
    for j in range(n_chan):
        inside = (place >= j * channels) & (place < (j + 1) * channels)
        weights = jnp.where(inside, mask_ref[chan, j].astype(jnp.float32), weights)
    out_ref[...] = own * (weights * float(seg * n_tm) ** (-0.5))

    to_right.wait_send()
    to_left.wait_send()
    for copy in gathers + near_copies + far_copies:
        copy.wait_send()


def shards(n_chan, n_tm, raw_strain, whitening, block_mask, old_stack):
    channels, seg = raw_strain.shape
    taps = whitening.shape[0]
    half = taps // 2
    lags = old_stack.shape[0]
    lag_total = lags * n_tm
    left = -(-lag_total // LANES) * LANES
    chips = n_tm // 2
    rows = channels * lags
    every = n_chan * channels
    width = taps + LANES
    windows = channels * (seg + left) // LANES
    dma = pltpu.SemaphoreType.DMA
    sums = pl.pallas_call(
        functools.partial(main_kernel, n_chan, n_tm, lag_total, half, left),
        out_shape=jax.ShapeDtypeStruct((rows, every), jnp.float32),
        in_specs=[
            pl.BlockSpec(memory_space=pl.ANY),
            pl.BlockSpec(memory_space=pltpu.VMEM),
            pl.BlockSpec(memory_space=pltpu.SMEM),
        ],
        out_specs=pl.BlockSpec(memory_space=pltpu.VMEM),
        scratch_shapes=[
            pltpu.VMEM((channels, seg), jnp.float32),
            pltpu.VMEM((channels, half + left), jnp.float32),
            pltpu.VMEM((channels, half), jnp.float32),
            pltpu.VMEM((windows, width), jnp.bfloat16),
            pltpu.VMEM((windows, width), jnp.bfloat16),
            pltpu.VMEM((channels, seg + left), jnp.float32),
            pltpu.VMEM((n_tm, rows, seg), jnp.bfloat16),
            pltpu.VMEM((n_chan, channels, seg), jnp.bfloat16),
            pltpu.VMEM((chips, rows, every), jnp.float32),
            pltpu.VMEM((chips, rows, every), jnp.float32),
            pltpu.VMEM((chips, rows, every), jnp.bfloat16),
            pltpu.VMEM((chips, rows, every), jnp.bfloat16),
            dma,
            dma((2,)),
            dma((2,)),
            dma((n_chan,)),
            dma((n_chan,)),
            dma((chips,)),
            dma((chips,)),
            dma((chips,)),
            dma((chips,)),
        ],
        compiler_params=pltpu.CompilerParams(
            collective_id=0, has_side_effects=True, vmem_limit_bytes=58 * 1024 * 1024
        ),
    )(raw_strain, whitening, block_mask)
    return old_stack + sums.reshape(lags, channels, every)


def solution(mesh):
    body = functools.partial(shards, mesh.shape["chan"], mesh.shape["tm"])
    in_specs = (P("chan", "tm"), P(), P(), P("tm", "chan", None))
    out_specs = P("tm", "chan", None)
    return jax.shard_map(body, mesh=mesh, in_specs=in_specs, out_specs=out_specs, check_vma=False)
```

```python
import functools

import jax
import jax.numpy as jnp
from jax import lax
from jax.experimental import pallas as pl
from jax.experimental.pallas import tpu as pltpu
from jax.sharding import PartitionSpec as P

MESH = pl.DeviceIdType.MESH
LANES = 128
NT = (((1,), (1,)), ((), ()))


def main_kernel(
    n_chan, n_tm, lag_total, half, left,
    raw_ref, taps_ref, mask_ref, out_ref,
    local, low_halo, high_halo, win_high, win_low, wide, stack, blocks, part, near, sent, far, mine,
    local_sem, halo_send, halo_recv, gather_send, gather_recv, near_send, near_recv, far_send, far_recv,
):
    chan, tm = lax.axis_index("chan"), lax.axis_index("tm")
    channels, seg = raw_ref.shape
    chips = n_tm // 2
    chip, core = tm // 2, lax.rem(tm, 2)
    lag_rows = channels * (lag_total // n_tm)

    own_copy = pltpu.make_async_copy(raw_ref, local, local_sem)
    own_copy.start()
    barrier = pltpu.get_barrier_semaphore()
    for d in range(1, n_tm):
        pl.semaphore_signal(
            barrier, inc=1, device_id=(chan, lax.rem(tm + d, n_tm)), device_id_type=MESH
        )
    for d in range(1, n_chan):
        pl.semaphore_signal(
            barrier, inc=1, device_id=(lax.rem(chan + d, n_chan), tm), device_id_type=MESH
        )
    pl.semaphore_wait(barrier, n_tm - 1 + n_chan - 1)

    to_right = pltpu.make_async_remote_copy(
        src_ref=raw_ref.at[:, pl.ds(seg - half - left, half + left)],
        dst_ref=low_halo,
        send_sem=halo_send.at[0],
        recv_sem=halo_recv.at[0],
        device_id=(chan, lax.rem(tm + 1, n_tm)),
        device_id_type=MESH,
    )
    to_left = pltpu.make_async_remote_copy(
        src_ref=raw_ref.at[:, pl.ds(0, half)],
        dst_ref=high_halo,
        send_sem=halo_send.at[1],
        recv_sem=halo_recv.at[1],
        device_id=(chan, lax.rem(tm + n_tm - 1, n_tm)),
        device_id_type=MESH,
    )
    to_right.start()
    to_left.start()

    width = 2 * half + LANES
    taps = jnp.concatenate(
        [taps_ref[...].reshape(1, 2 * half), jnp.zeros((1, LANES), jnp.float32)], axis=1
    )
    matrix = pltpu.roll(
        jnp.broadcast_to(taps, (LANES, width)), 0, 1, stride=1, stride_axis=0
    )
    matrix_high = matrix.astype(jnp.bfloat16)
    matrix_low = (matrix - matrix_high.astype(jnp.float32)).astype(jnp.bfloat16)
    matrix_both = jnp.concatenate([matrix_high, matrix_low], axis=0)

    own_copy.wait()
    to_right.wait_recv()
    to_left.wait_recv()
    not_first = (tm > 0).astype(jnp.float32)
    not_last = (tm < n_tm - 1).astype(jnp.float32)
    padded = jnp.concatenate(
        [low_halo[...] * not_first, local[...], high_halo[...] * not_last], axis=1
    )
    high = padded.astype(jnp.bfloat16)
    low = (padded - high.astype(jnp.float32)).astype(jnp.bfloat16)
    pieces = (seg + left) // LANES
    for b in range(pieces):
        win_high[pl.ds(b * channels, channels)] = high[:, b * LANES : b * LANES + width]
        win_low[pl.ds(b * channels, channels)] = low[:, b * LANES : b * LANES + width]
    both = lax.dot_general(
        win_high[...], matrix_both, NT, preferred_element_type=jnp.float32
    )
    rest = lax.dot_general(
        win_low[...], matrix_high, NT, preferred_element_type=jnp.float32
    )
    total = both[:, :LANES] + (both[:, LANES:] + rest)
    rounded = total.astype(jnp.bfloat16)
    ahead = left // LANES
    for b in range(ahead, pieces):
        blocks[chan, :, pl.ds((b - ahead) * LANES, LANES)] = rounded[
            b * channels : (b + 1) * channels
        ]

    last = n_chan - 1

    def hop(step, way):
        lane = 0 if way > 0 else 1

        def copy(block):
            return pltpu.make_async_remote_copy(
                src_ref=blocks.at[block],
                dst_ref=blocks.at[block],
                send_sem=gather_send.at[lane, step],
                recv_sem=gather_recv.at[lane, step],
                device_id=(lax.rem(chan + way + n_chan, n_chan), tm),
                device_id_type=MESH,
            )

        if way > 0:
            sends = (chan >= step) & (chan < last)
            gets = chan >= step + 1
        else:
            sends = (chan <= last - step) & (chan > 0)
            gets = chan <= last - 1 - step
        return copy, sends, chan - way * step, gets, chan - way * (step + 1)

    def start_hops(step):
        for way in (1, -1):
            copy, sends, block, _, _ = hop(step, way)

            @pl.when(sends)
            def _():
                copy(block).start()

    def finish_hops(step):
        for way in (1, -1):
            copy, _, _, gets, block = hop(step, way)

            @pl.when(gets)
            def _():
                copy(block).wait_recv()

    def sent_hops(step):
        for way in (1, -1):
            copy, sends, block, _, _ = hop(step, way)

            @pl.when(sends)
            def _():
                copy(block).wait_send()

    start_hops(0)

    exact = rounded.astype(jnp.float32)
    for b in range(pieces):
        piece = exact[b * channels : (b + 1) * channels]
        wide[:, pl.ds(b * LANES, LANES)] = piece * not_first if b < ahead else piece
    for lag in range(lag_total):
        q, row = divmod(lag * channels, lag_rows)
        moved = wide[...] if lag == 0 else pltpu.roll(wide[...], lag, 1)
        stack[q, pl.ds(row, channels)] = moved[:, left:].astype(jnp.bfloat16)
    finish_hops(0)
    if n_chan > 2:
        start_hops(1)

    rounds = n_chan // 2
    span = 2 * channels
    near_copies, far_copies = [], []

    def pair_of(turn):
        return lax.rem(chan // 2 + turn, rounds)

    def partners(turn):
        return blocks[pl.ds(2 * pair_of(turn), 2)].reshape(span, seg)

    def partial_sums(q, partner):
        return lax.dot_general(stack[q], partner, NT, preferred_element_type=jnp.float32)

    def send_near(turn):
        partner = partners(turn)
        for d in range(chips):
            owner = lax.rem(chip + d + 1, chips)
            slot = turn * chips + d
            part[slot] = partial_sums(owner * 2 + 1 - core, partner)
            near_copies.append(
                pltpu.make_async_remote_copy(
                    src_ref=part.at[slot],
                    dst_ref=near.at[slot],
                    send_sem=near_send.at[slot],
                    recv_sem=near_recv.at[slot],
                    device_id=(chan, chip * 2 + 1 - core),
                    device_id_type=MESH,
                )
            )
            near_copies[-1].start()

    def send_far(turn):
        partner = partners(turn)
        for d in range(chips):
            owner = lax.rem(chip + d + 1, chips)
            slot = turn * chips + d
            own = partial_sums(owner * 2 + core, partner)
            near_copies[slot].wait_recv()
            if d == chips - 1:
                return own + near[slot]
            sent[slot] = (own + near[slot]).astype(jnp.bfloat16)
            far_copies.append(
                pltpu.make_async_remote_copy(
                    src_ref=sent.at[slot],
                    dst_ref=far.at[slot],
                    send_sem=far_send.at[slot],
                    recv_sem=far_recv.at[slot],
                    device_id=(chan, owner * 2 + core),
                    device_id_type=MESH,
                )
            )
            far_copies[-1].start()

    for turn in range(rounds):
        send_near(turn)
        if turn == 0 and n_chan > 2:
            finish_hops(1)
            if n_chan > 3:
                start_hops(2)
        mine[turn] = send_far(turn)
        if turn == 0:
            for step in range(2, n_chan - 1):
                finish_hops(step)
                if step + 1 < n_chan - 1:
                    start_hops(step + 1)

    for turn in range(rounds):
        own = mine[turn]
        for d in range(chips - 1):
            far_copies[turn * (chips - 1) + d].wait_recv()
            own = own + far[turn * chips + d].astype(jnp.float32)
        pair = pair_of(turn)
        place = lax.broadcasted_iota(jnp.int32, (1, span), 1)
        weights = jnp.where(
            place < channels,
            mask_ref[chan, 2 * pair].astype(jnp.float32),
            mask_ref[chan, 2 * pair + 1].astype(jnp.float32),
        )
        columns = pl.ds(pl.multiple_of(pair * span, span), span)
        out_ref[:, columns] = own * (weights * float(seg * n_tm) ** (-0.5))

    to_right.wait_send()
    to_left.wait_send()
    for step in range(n_chan - 1):
        sent_hops(step)
    for copy in near_copies + far_copies:
        copy.wait_send()


def shards(n_chan, n_tm, raw_strain, whitening, block_mask, old_stack):
    channels, seg = raw_strain.shape
    taps = whitening.shape[0]
    half = taps // 2
    lags = old_stack.shape[0]
    lag_total = lags * n_tm
    left = -(-lag_total // LANES) * LANES
    chips = n_tm // 2
    rows = channels * lags
    every = n_chan * channels
    span = 2 * channels
    slots = chips * (n_chan // 2)
    width = taps + LANES
    windows = channels * (seg + left) // LANES
    dma = pltpu.SemaphoreType.DMA
    sums = pl.pallas_call(
        functools.partial(main_kernel, n_chan, n_tm, lag_total, half, left),
        out_shape=jax.ShapeDtypeStruct((rows, every), jnp.float32),
        in_specs=[
            pl.BlockSpec(memory_space=pl.ANY),
            pl.BlockSpec(memory_space=pltpu.VMEM),
            pl.BlockSpec(memory_space=pltpu.SMEM),
        ],
        out_specs=pl.BlockSpec(memory_space=pltpu.VMEM),
        scratch_shapes=[
            pltpu.VMEM((channels, seg), jnp.float32),
            pltpu.VMEM((channels, half + left), jnp.float32),
            pltpu.VMEM((channels, half), jnp.float32),
            pltpu.VMEM((windows, width), jnp.bfloat16),
            pltpu.VMEM((windows, width), jnp.bfloat16),
            pltpu.VMEM((channels, seg + left), jnp.float32),
            pltpu.VMEM((n_tm, rows, seg), jnp.bfloat16),
            pltpu.VMEM((n_chan, channels, seg), jnp.bfloat16),
            pltpu.VMEM((slots, rows, span), jnp.float32),
            pltpu.VMEM((slots, rows, span), jnp.float32),
            pltpu.VMEM((slots, rows, span), jnp.bfloat16),
            pltpu.VMEM((slots, rows, span), jnp.bfloat16),
            pltpu.VMEM((n_chan // 2, rows, span), jnp.float32),
            dma,
            dma((2,)),
            dma((2,)),
            dma((2, n_chan)),
            dma((2, n_chan)),
            dma((slots,)),
            dma((slots,)),
            dma((slots,)),
            dma((slots,)),
        ],
        compiler_params=pltpu.CompilerParams(
            collective_id=0, has_side_effects=True, vmem_limit_bytes=58 * 1024 * 1024
        ),
    )(raw_strain, whitening, block_mask)
    return old_stack + sums.reshape(lags, channels, every)


def solution(mesh):
    body = functools.partial(shards, mesh.shape["chan"], mesh.shape["tm"])
    in_specs = (P("chan", "tm"), P(), P(), P("tm", "chan", None))
    out_specs = P("tm", "chan", None)
    return jax.shard_map(body, mesh=mesh, in_specs=in_specs, out_specs=out_specs, check_vma=False)
```

```python
import functools

import jax
import jax.numpy as jnp
from jax import lax
from jax.experimental import pallas as pl
from jax.experimental.pallas import tpu as pltpu
from jax.sharding import PartitionSpec as P

MESH = pl.DeviceIdType.MESH
LANES = 128
NT = (((1,), (1,)), ((), ()))


def main_kernel(
    n_chan, n_tm, lag_total, half, left,
    raw_ref, taps_ref, mask_ref, out_ref,
    local, low_halo, high_halo, win_high, win_low, wide, stack, blocks, part, near, sent, far, mine,
    local_sem, halo_send, halo_recv, gather_send, gather_recv, near_send, near_recv, far_send, far_recv,
):
    chan, tm = lax.axis_index("chan"), lax.axis_index("tm")
    channels, seg = raw_ref.shape
    chips = n_tm // 2
    chip, core = tm // 2, lax.rem(tm, 2)
    lag_rows = channels * (lag_total // n_tm)

    own_copy = pltpu.make_async_copy(raw_ref, local, local_sem)
    own_copy.start()
    def other_chip(d):
        offset, result, bit = chips - 1 - d, 0, 1
        while bit < chips:
            result = result + bit * lax.rem(chip // bit + offset // bit % 2, 2)
            bit *= 2
        return result

    barrier = pltpu.get_barrier_semaphore()
    for d in range(1, n_tm):
        pl.semaphore_signal(
            barrier, inc=1, device_id=(chan, lax.rem(tm + d, n_tm)), device_id_type=MESH
        )
    for d in range(1, n_chan):
        pl.semaphore_signal(
            barrier, inc=1, device_id=(lax.rem(chan + d, n_chan), tm), device_id_type=MESH
        )
    pl.semaphore_wait(barrier, n_tm - 1 + n_chan - 1)

    to_right = pltpu.make_async_remote_copy(
        src_ref=raw_ref.at[:, pl.ds(seg - half - left, half + left)],
        dst_ref=low_halo,
        send_sem=halo_send.at[0],
        recv_sem=halo_recv.at[0],
        device_id=(chan, lax.rem(tm + 1, n_tm)),
        device_id_type=MESH,
    )
    to_left = pltpu.make_async_remote_copy(
        src_ref=raw_ref.at[:, pl.ds(0, half)],
        dst_ref=high_halo,
        send_sem=halo_send.at[1],
        recv_sem=halo_recv.at[1],
        device_id=(chan, lax.rem(tm + n_tm - 1, n_tm)),
        device_id_type=MESH,
    )
    to_right.start()
    to_left.start()

    width = 2 * half + LANES
    taps = jnp.concatenate(
        [taps_ref[...].reshape(1, 2 * half), jnp.zeros((1, LANES), jnp.float32)], axis=1
    )
    matrix = pltpu.roll(
        jnp.broadcast_to(taps, (LANES, width)), 0, 1, stride=1, stride_axis=0
    )
    matrix_high = matrix.astype(jnp.bfloat16)
    matrix_low = (matrix - matrix_high.astype(jnp.float32)).astype(jnp.bfloat16)
    matrix_both = jnp.concatenate([matrix_high, matrix_low], axis=0)

    own_copy.wait()
    to_right.wait_recv()
    to_left.wait_recv()
    not_first = (tm > 0).astype(jnp.float32)
    not_last = (tm < n_tm - 1).astype(jnp.float32)
    padded = jnp.concatenate(
        [low_halo[...] * not_first, local[...], high_halo[...] * not_last], axis=1
    )
    high = padded.astype(jnp.bfloat16)
    low = (padded - high.astype(jnp.float32)).astype(jnp.bfloat16)
    pieces = (seg + left) // LANES
    for b in range(pieces):
        win_high[pl.ds(b * channels, channels)] = high[:, b * LANES : b * LANES + width]
        win_low[pl.ds(b * channels, channels)] = low[:, b * LANES : b * LANES + width]
    both = lax.dot_general(
        win_high[...], matrix_both, NT, preferred_element_type=jnp.float32
    )
    rest = lax.dot_general(
        win_low[...], matrix_high, NT, preferred_element_type=jnp.float32
    )
    total = both[:, :LANES] + (both[:, LANES:] + rest)
    rounded = total.astype(jnp.bfloat16)
    ahead = left // LANES
    for b in range(ahead, pieces):
        blocks[chan, :, pl.ds((b - ahead) * LANES, LANES)] = rounded[
            b * channels : (b + 1) * channels
        ]

    last = n_chan - 1

    pieces_of = 4 if channels % 64 == 0 else 1
    depth = channels // pieces_of

    def hop(step, way, piece):
        rows = pl.ds(piece * depth, depth)
        lane = 0 if way > 0 else 1

        def copy(block):
            return pltpu.make_async_remote_copy(
                src_ref=blocks.at[block, rows],
                dst_ref=blocks.at[block, rows],
                send_sem=gather_send.at[lane, step, piece],
                recv_sem=gather_recv.at[lane, step, piece],
                device_id=(lax.rem(chan + way + n_chan, n_chan), tm),
                device_id_type=MESH,
            )

        if way > 0:
            sends = (chan >= step) & (chan < last)
            gets = chan >= step + 1
        else:
            sends = (chan <= last - step) & (chan > 0)
            gets = chan <= last - 1 - step
        return copy, sends, chan - way * step, gets, chan - way * (step + 1)

    def start_hops(step, piece):
        for way in (1, -1):
            copy, sends, block, _, _ = hop(step, way, piece)

            @pl.when(sends)
            def _():
                copy(block).start()

    def finish_hops(step, piece):
        for way in (1, -1):
            copy, _, _, gets, block = hop(step, way, piece)

            @pl.when(gets)
            def _():
                copy(block).wait_recv()

    def sent_hops(step, piece):
        for way in (1, -1):
            copy, sends, block, _, _ = hop(step, way, piece)

            @pl.when(sends)
            def _():
                copy(block).wait_send()

    def hand_on(step):
        for piece in range(pieces_of):
            finish_hops(step, piece)
            if step + 1 < n_chan - 1:
                start_hops(step + 1, piece)

    for piece in range(pieces_of):
        start_hops(0, piece)

    exact = rounded.astype(jnp.float32)
    for b in range(pieces):
        piece = exact[b * channels : (b + 1) * channels]
        wide[:, pl.ds(b * LANES, LANES)] = piece * not_first if b < ahead else piece
    for lag in range(lag_total):
        q, row = divmod(lag * channels, lag_rows)
        moved = wide[...] if lag == 0 else pltpu.roll(wide[...], lag, 1)
        stack[q, pl.ds(row, channels)] = moved[:, left:].astype(jnp.bfloat16)
    hand_on(0)

    rounds = n_chan // 2
    span = 2 * channels
    near_copies, far_copies = [], []

    def pair_of(turn):
        return lax.rem(chan // 2 + turn, rounds)

    def partners(turn):
        return blocks[pl.ds(2 * pair_of(turn), 2)].reshape(span, seg)

    def partial_sums(q, partner):
        return lax.dot_general(stack[q], partner, NT, preferred_element_type=jnp.float32)

    def send_near(turn):
        partner = partners(turn)
        for d in range(chips):
            owner = other_chip(d)
            slot = turn * chips + d
            part[slot] = partial_sums(owner * 2 + 1 - core, partner)
            near_copies.append(
                pltpu.make_async_remote_copy(
                    src_ref=part.at[slot],
                    dst_ref=near.at[slot],
                    send_sem=near_send.at[slot],
                    recv_sem=near_recv.at[slot],
                    device_id=(chan, chip * 2 + 1 - core),
                    device_id_type=MESH,
                )
            )
            near_copies[-1].start()

    def send_far(turn):
        partner = partners(turn)
        for d in range(chips):
            owner = other_chip(d)
            slot = turn * chips + d
            own = partial_sums(owner * 2 + core, partner)
            near_copies[slot].wait_recv()
            if d == chips - 1:
                return own + near[slot]
            sent[slot] = (own + near[slot]).astype(jnp.bfloat16)
            far_copies.append(
                pltpu.make_async_remote_copy(
                    src_ref=sent.at[slot],
                    dst_ref=far.at[slot],
                    send_sem=far_send.at[slot],
                    recv_sem=far_recv.at[slot],
                    device_id=(chan, owner * 2 + core),
                    device_id_type=MESH,
                )
            )
            far_copies[-1].start()

    for turn in range(rounds):
        send_near(turn)
        if turn == 0 and n_chan > 2:
            hand_on(1)
        mine[turn] = send_far(turn)
        if turn == 0:
            for step in range(2, n_chan - 1):
                hand_on(step)

    for turn in range(rounds):
        own = mine[turn]
        for d in range(chips - 1):
            far_copies[turn * (chips - 1) + d].wait_recv()
            own = own + far[turn * chips + d].astype(jnp.float32)
        pair = pair_of(turn)
        place = lax.broadcasted_iota(jnp.int32, (1, span), 1)
        weights = jnp.where(
            place < channels,
            mask_ref[chan, 2 * pair].astype(jnp.float32),
            mask_ref[chan, 2 * pair + 1].astype(jnp.float32),
        )
        columns = pl.ds(pl.multiple_of(pair * span, span), span)
        out_ref[:, columns] = own * (weights * float(seg * n_tm) ** (-0.5))

    to_right.wait_send()
    to_left.wait_send()
    for step in range(n_chan - 1):
        for piece in range(pieces_of):
            sent_hops(step, piece)
    for copy in near_copies + far_copies:
        copy.wait_send()


def shards(n_chan, n_tm, raw_strain, whitening, block_mask, old_stack):
    channels, seg = raw_strain.shape
    taps = whitening.shape[0]
    half = taps // 2
    lags = old_stack.shape[0]
    lag_total = lags * n_tm
    left = -(-lag_total // LANES) * LANES
    chips = n_tm // 2
    rows = channels * lags
    every = n_chan * channels
    span = 2 * channels
    slots = chips * (n_chan // 2)
    width = taps + LANES
    windows = channels * (seg + left) // LANES
    dma = pltpu.SemaphoreType.DMA
    sums = pl.pallas_call(
        functools.partial(main_kernel, n_chan, n_tm, lag_total, half, left),
        out_shape=jax.ShapeDtypeStruct((rows, every), jnp.float32),
        in_specs=[
            pl.BlockSpec(memory_space=pl.ANY),
            pl.BlockSpec(memory_space=pltpu.VMEM),
            pl.BlockSpec(memory_space=pltpu.SMEM),
        ],
        out_specs=pl.BlockSpec(memory_space=pltpu.VMEM),
        scratch_shapes=[
            pltpu.VMEM((channels, seg), jnp.float32),
            pltpu.VMEM((channels, half + left), jnp.float32),
            pltpu.VMEM((channels, half), jnp.float32),
            pltpu.VMEM((windows, width), jnp.bfloat16),
            pltpu.VMEM((windows, width), jnp.bfloat16),
            pltpu.VMEM((channels, seg + left), jnp.float32),
            pltpu.VMEM((n_tm, rows, seg), jnp.bfloat16),
            pltpu.VMEM((n_chan, channels, seg), jnp.bfloat16),
            pltpu.VMEM((slots, rows, span), jnp.float32),
            pltpu.VMEM((slots, rows, span), jnp.float32),
            pltpu.VMEM((slots, rows, span), jnp.bfloat16),
            pltpu.VMEM((slots, rows, span), jnp.bfloat16),
            pltpu.VMEM((n_chan // 2, rows, span), jnp.float32),
            dma,
            dma((2,)),
            dma((2,)),
            dma((2, n_chan, 4)),
            dma((2, n_chan, 4)),
            dma((slots,)),
            dma((slots,)),
            dma((slots,)),
            dma((slots,)),
        ],
        compiler_params=pltpu.CompilerParams(
            collective_id=0, has_side_effects=True, vmem_limit_bytes=58 * 1024 * 1024
        ),
    )(raw_strain, whitening, block_mask)
    return old_stack + sums.reshape(lags, channels, every)


def solution(mesh):
    body = functools.partial(shards, mesh.shape["chan"], mesh.shape["tm"])
    in_specs = (P("chan", "tm"), P(), P(), P("tm", "chan", None))
    out_specs = P("tm", "chan", None)
    return jax.shard_map(body, mesh=mesh, in_specs=in_specs, out_specs=out_specs, check_vma=False)
```

```python
import functools

import jax
import jax.numpy as jnp
from jax import lax
from jax.experimental import pallas as pl
from jax.experimental.pallas import tpu as pltpu
from jax.sharding import PartitionSpec as P

MESH = pl.DeviceIdType.MESH
LANES = 128
NT = (((1,), (1,)), ((), ()))


def main_kernel(
    n_chan, n_tm, lag_total, half, left,
    raw_ref, taps_ref, mask_ref, out_ref,
    local, low_halo, high_halo, win_high, win_low, wide, stack, blocks, part, near, sent, far, mine,
    local_sem, halo_send, halo_recv, gather_send, gather_recv, near_send, near_recv, far_send, far_recv,
):
    chan, tm = lax.axis_index("chan"), lax.axis_index("tm")
    channels, seg = raw_ref.shape
    chips = n_tm // 2
    chip, core = tm // 2, lax.rem(tm, 2)
    lag_rows = channels * (lag_total // n_tm)

    own_copy = pltpu.make_async_copy(raw_ref, local, local_sem)
    own_copy.start()
    def other_chip(d):
        offset, result, bit = chips - 1 - d, 0, 1
        while bit < chips:
            result = result + bit * lax.rem(chip // bit + offset // bit % 2, 2)
            bit *= 2
        return result

    barrier = pltpu.get_barrier_semaphore()
    last = n_chan - 1
    others = [lax.rem(tm + 1, n_tm), lax.rem(tm + n_tm - 1, n_tm)]
    others += [other_chip(d) * 2 + core for d in range(chips - 1)]
    for other in others:
        pl.semaphore_signal(barrier, inc=1, device_id=(chan, other), device_id_type=MESH)

    @pl.when(chan > 0)
    def _():
        pl.semaphore_signal(barrier, inc=1, device_id=(chan - 1, tm), device_id_type=MESH)

    @pl.when(chan < last)
    def _():
        pl.semaphore_signal(barrier, inc=1, device_id=(chan + 1, tm), device_id_type=MESH)

    beside = (chan > 0).astype(jnp.int32) + (chan < last).astype(jnp.int32)
    pl.semaphore_wait(barrier, len(others) + beside)

    to_right = pltpu.make_async_remote_copy(
        src_ref=raw_ref.at[:, pl.ds(seg - half - left, half + left)],
        dst_ref=low_halo,
        send_sem=halo_send.at[0],
        recv_sem=halo_recv.at[0],
        device_id=(chan, lax.rem(tm + 1, n_tm)),
        device_id_type=MESH,
    )
    to_left = pltpu.make_async_remote_copy(
        src_ref=raw_ref.at[:, pl.ds(0, half)],
        dst_ref=high_halo,
        send_sem=halo_send.at[1],
        recv_sem=halo_recv.at[1],
        device_id=(chan, lax.rem(tm + n_tm - 1, n_tm)),
        device_id_type=MESH,
    )
    @pl.when(tm < n_tm - 1)
    def _():
        to_right.start()

    @pl.when(tm > 0)
    def _():
        to_left.start()

    width = 2 * half + LANES
    taps = jnp.concatenate(
        [taps_ref[...].reshape(1, 2 * half), jnp.zeros((1, LANES), jnp.float32)], axis=1
    )
    matrix = pltpu.roll(
        jnp.broadcast_to(taps, (LANES, width)), 0, 1, stride=1, stride_axis=0
    )
    matrix_high = matrix.astype(jnp.bfloat16)
    matrix_low = (matrix - matrix_high.astype(jnp.float32)).astype(jnp.bfloat16)
    matrix_both = jnp.concatenate([matrix_high, matrix_low], axis=0)

    own_copy.wait()

    @pl.when(tm > 0)
    def _():
        to_right.wait_recv()

    @pl.when(tm == 0)
    def _():
        low_halo[...] = jnp.zeros_like(low_halo)

    @pl.when(tm < n_tm - 1)
    def _():
        to_left.wait_recv()

    @pl.when(tm == n_tm - 1)
    def _():
        high_halo[...] = jnp.zeros_like(high_halo)

    not_first = (tm > 0).astype(jnp.float32)
    padded = jnp.concatenate(
        [low_halo[...], local[...], high_halo[...]], axis=1
    )
    high = padded.astype(jnp.bfloat16)
    low = (padded - high.astype(jnp.float32)).astype(jnp.bfloat16)
    pieces = (seg + left) // LANES
    for b in range(pieces):
        win_high[pl.ds(b * channels, channels)] = high[:, b * LANES : b * LANES + width]
        win_low[pl.ds(b * channels, channels)] = low[:, b * LANES : b * LANES + width]
    both = lax.dot_general(
        win_high[...], matrix_both, NT, preferred_element_type=jnp.float32
    )
    rest = lax.dot_general(
        win_low[...], matrix_high, NT, preferred_element_type=jnp.float32
    )
    total = both[:, :LANES] + (both[:, LANES:] + rest)
    rounded = total.astype(jnp.bfloat16)
    ahead = left // LANES
    for b in range(ahead, pieces):
        blocks[chan, :, pl.ds((b - ahead) * LANES, LANES)] = rounded[
            b * channels : (b + 1) * channels
        ]

    last = n_chan - 1

    pieces_of = 4 if channels % 64 == 0 else 1
    depth = channels // pieces_of

    def hop(step, way, piece):
        rows = pl.ds(piece * depth, depth)
        lane = 0 if way > 0 else 1

        def copy(block):
            return pltpu.make_async_remote_copy(
                src_ref=blocks.at[block, rows],
                dst_ref=blocks.at[block, rows],
                send_sem=gather_send.at[lane, step, piece],
                recv_sem=gather_recv.at[lane, step, piece],
                device_id=(lax.rem(chan + way + n_chan, n_chan), tm),
                device_id_type=MESH,
            )

        if way > 0:
            sends = (chan >= step) & (chan < last)
            gets = chan >= step + 1
        else:
            sends = (chan <= last - step) & (chan > 0)
            gets = chan <= last - 1 - step
        return copy, sends, chan - way * step, gets, chan - way * (step + 1)

    def start_hops(step, piece):
        for way in (1, -1):
            copy, sends, block, _, _ = hop(step, way, piece)

            @pl.when(sends)
            def _():
                copy(block).start()

    def finish_hops(step, piece):
        for way in (1, -1):
            copy, _, _, gets, block = hop(step, way, piece)

            @pl.when(gets)
            def _():
                copy(block).wait_recv()

    def sent_hops(step, piece):
        for way in (1, -1):
            copy, sends, block, _, _ = hop(step, way, piece)

            @pl.when(sends)
            def _():
                copy(block).wait_send()

    def hand_on_piece(step, piece):
        finish_hops(step, piece)
        if step + 1 < n_chan - 1:
            start_hops(step + 1, piece)

    def hand_on(step):
        for piece in range(pieces_of):
            hand_on_piece(step, piece)

    for piece in range(pieces_of):
        start_hops(0, piece)

    exact = rounded.astype(jnp.float32)
    for b in range(pieces):
        piece = exact[b * channels : (b + 1) * channels]
        wide[:, pl.ds(b * LANES, LANES)] = piece * not_first if b < ahead else piece
    for lag in range(lag_total):
        q, row = divmod(lag * channels, lag_rows)
        moved = wide[...] if lag == 0 else pltpu.roll(wide[...], lag, 1)
        stack[q, pl.ds(row, channels)] = moved[:, left:].astype(jnp.bfloat16)
        if (lag + 1) * pieces_of % lag_total == 0:
            hand_on_piece(0, (lag + 1) * pieces_of // lag_total - 1)

    rounds = n_chan // 2
    span = 2 * channels
    near_copies, far_copies = [], []

    def pair_of(turn):
        return lax.rem(chan // 2 + turn, rounds)

    def partners(turn):
        return blocks[pl.ds(2 * pair_of(turn), 2)].reshape(span, seg)

    def partial_sums(q, partner):
        return lax.dot_general(stack[q], partner, NT, preferred_element_type=jnp.float32)

    def send_near(turn):
        partner = partners(turn)
        for d in range(chips):
            owner = other_chip(d)
            slot = turn * chips + d
            part[slot] = partial_sums(owner * 2 + 1 - core, partner)
            near_copies.append(
                pltpu.make_async_remote_copy(
                    src_ref=part.at[slot],
                    dst_ref=near.at[slot],
                    send_sem=near_send.at[slot],
                    recv_sem=near_recv.at[slot],
                    device_id=(chan, chip * 2 + 1 - core),
                    device_id_type=MESH,
                )
            )
            near_copies[-1].start()

    def send_far(turn):
        partner = partners(turn)
        for d in range(chips):
            owner = other_chip(d)
            slot = turn * chips + d
            own = partial_sums(owner * 2 + core, partner)
            near_copies[slot].wait_recv()
            if d == chips - 1:
                return own + near[slot]
            sent[slot] = (own + near[slot]).astype(jnp.bfloat16)
            far_copies.append(
                pltpu.make_async_remote_copy(
                    src_ref=sent.at[slot],
                    dst_ref=far.at[slot],
                    send_sem=far_send.at[slot],
                    recv_sem=far_recv.at[slot],
                    device_id=(chan, owner * 2 + core),
                    device_id_type=MESH,
                )
            )
            far_copies[-1].start()

    for turn in range(rounds):
        send_near(turn)
        if turn == 0 and n_chan > 2:
            hand_on(1)
        mine[turn] = send_far(turn)
        if turn == 0:
            for step in range(2, n_chan - 1):
                hand_on(step)

    for turn in range(rounds):
        own = mine[turn]
        for d in range(chips - 1):
            far_copies[turn * (chips - 1) + d].wait_recv()
            own = own + far[turn * chips + d].astype(jnp.float32)
        pair = pair_of(turn)
        place = lax.broadcasted_iota(jnp.int32, (1, span), 1)
        weights = jnp.where(
            place < channels,
            mask_ref[chan, 2 * pair].astype(jnp.float32),
            mask_ref[chan, 2 * pair + 1].astype(jnp.float32),
        )
        columns = pl.ds(pl.multiple_of(pair * span, span), span)
        out_ref[:, columns] = own * (weights * float(seg * n_tm) ** (-0.5))

    @pl.when(tm < n_tm - 1)
    def _():
        to_right.wait_send()

    @pl.when(tm > 0)
    def _():
        to_left.wait_send()

    for step in range(n_chan - 1):
        for piece in range(pieces_of):
            sent_hops(step, piece)
    for copy in near_copies + far_copies:
        copy.wait_send()


def shards(n_chan, n_tm, raw_strain, whitening, block_mask, old_stack):
    channels, seg = raw_strain.shape
    taps = whitening.shape[0]
    half = taps // 2
    lags = old_stack.shape[0]
    lag_total = lags * n_tm
    left = -(-lag_total // LANES) * LANES
    chips = n_tm // 2
    rows = channels * lags
    every = n_chan * channels
    span = 2 * channels
    slots = chips * (n_chan // 2)
    width = taps + LANES
    windows = channels * (seg + left) // LANES
    dma = pltpu.SemaphoreType.DMA
    sums = pl.pallas_call(
        functools.partial(main_kernel, n_chan, n_tm, lag_total, half, left),
        out_shape=jax.ShapeDtypeStruct((rows, every), jnp.float32),
        in_specs=[
            pl.BlockSpec(memory_space=pl.ANY),
            pl.BlockSpec(memory_space=pltpu.VMEM),
            pl.BlockSpec(memory_space=pltpu.SMEM),
        ],
        out_specs=pl.BlockSpec(memory_space=pltpu.VMEM),
        scratch_shapes=[
            pltpu.VMEM((channels, seg), jnp.float32),
            pltpu.VMEM((channels, half + left), jnp.float32),
            pltpu.VMEM((channels, half), jnp.float32),
            pltpu.VMEM((windows, width), jnp.bfloat16),
            pltpu.VMEM((windows, width), jnp.bfloat16),
            pltpu.VMEM((channels, seg + left), jnp.float32),
            pltpu.VMEM((n_tm, rows, seg), jnp.bfloat16),
            pltpu.VMEM((n_chan, channels, seg), jnp.bfloat16),
            pltpu.VMEM((slots, rows, span), jnp.float32),
            pltpu.VMEM((slots, rows, span), jnp.float32),
            pltpu.VMEM((slots, rows, span), jnp.bfloat16),
            pltpu.VMEM((slots, rows, span), jnp.bfloat16),
            pltpu.VMEM((n_chan // 2, rows, span), jnp.float32),
            dma,
            dma((2,)),
            dma((2,)),
            dma((2, n_chan, 4)),
            dma((2, n_chan, 4)),
            dma((slots,)),
            dma((slots,)),
            dma((slots,)),
            dma((slots,)),
        ],
        compiler_params=pltpu.CompilerParams(
            collective_id=0, has_side_effects=True, vmem_limit_bytes=58 * 1024 * 1024
        ),
    )(raw_strain, whitening, block_mask)
    return old_stack + sums.reshape(lags, channels, every)


def solution(mesh):
    body = functools.partial(shards, mesh.shape["chan"], mesh.shape["tm"])
    in_specs = (P("chan", "tm"), P(), P(), P("tm", "chan", None))
    out_specs = P("tm", "chan", None)
    return jax.shard_map(body, mesh=mesh, in_specs=in_specs, out_specs=out_specs, check_vma=False)
```
